32 devices in a mesh: row: 4 (over x, core), col: 8 (over z, y).
Axes of the slice: x: 2, y: 2, z: 4, core: 2. Of those that a mesh axis runs over, the one named last changes fastest.
Arguments:
- inputs: bfloat16 [128, 8192], P('col', 'row'), may hold values from -6 to 6
- out_grad: bfloat16 [128, 8192], P('col', 'row'), may hold values from -0.8984375 to 0.8984375
- gate_pre: bfloat16 [128, 16384], P('row', 'col'), may hold values from -6 to 6
- up_pre: bfloat16 [128, 16384], P('row', 'col'), may hold values from -6 to 6
- gate_weight: bfloat16 [8192, 16384], P('row', 'col'), may hold values from -0.0625 to 0.0625
- up_weight: bfloat16 [8192, 16384], P('row', 'col'), may hold values from -0.0625 to 0.0625
- down_weight: bfloat16 [16384, 8192], P('col', 'row'), may hold values from -0.0625 to 0.0625
Outputs:
- input_grad: bfloat16 [128, 8192], P('col', 'row')
- gate_grad: bfloat16 [8192, 16384], P('row', 'col')
- up_grad: bfloat16 [8192, 16384], P('row', 'col')
- down_grad: bfloat16 [16384, 8192], P('col', 'row')
The draws below stay inside these ranges and needn't reach their ends.
All inputs are finite; a program needn't handle non-finite values.
Results may differ from the reference program's by a relative error of at most 0.028.
Values may be sent and summed in bfloat16 or wider, within the bound.
A program may use at most 128 MiB of HBM per device.

```python
import jax
import jax.numpy as jnp
from jax import lax

D = 8192
FF = 16384
TOKENS = 128
D_BLK = 2048
FF_BLK = 2048
N_ROW = 4
N_COL = 8


def strengthened(array, own_key, source, target, blocks, factor):
    def block_of(position):
        return (jnp.arange(array.shape[position]) // (array.shape[position] // blocks)).reshape((-1,) + (1,) * (array.ndim - 1 - position))

    first = jax.random.permutation(own_key, blocks)[block_of(target)]
    second = (block_of(target) + blocks // 2) % blocks
    return jnp.where((block_of(source) == first) | (block_of(source) == second), factor * array, array)


def levels(own_key, shape, shards, smallest, top_value):
    loudness = 1.0
    for position, shards_of in shards:
        heights = jax.random.uniform(jax.random.fold_in(jax.random.fold_in(own_key, 6), position), (shards_of,), jnp.float32, smallest / len(shards), top_value / len(shards))
        loudness = loudness * jnp.repeat(jnp.exp(heights), shape[position] // shards_of).reshape((-1,) + (1,) * (len(shape) - 1 - position))
    return loudness


def scatter_about(stream_key, dims, deviation, bound, shards=(), kind=jnp.bfloat16):
    level = levels(stream_key, dims, shards, -0.22, 0.18) if shards else 1.0
    result = jax.random.normal(stream_key, dims, jnp.float32) * deviation * level
    return jnp.minimum(jnp.maximum(result, -bound), bound).astype(kind)


def noise_with(own_key, extent, spread, most, pieces, heavy, kind=jnp.bfloat16):
    result = spread * jax.random.normal(own_key, extent, jnp.float32)
    if pieces:
        result = result * levels(own_key, extent, pieces, -0.22, 0.18)
    return jnp.clip(strengthened(result, jax.random.fold_in(own_key, 3), *heavy), -most, most).astype(kind)


def setup_inputs(seed: int = 0) -> dict:
    splits = jax.random.split(jax.random.key(seed), 8)
    inputs = scatter_about(splits[0], (TOKENS, D), 1.0, 6.0, ((0, 8), (1, 4)))
    out_grad = noise_with(splits[1], (TOKENS, D), 0.15, 0.8984375, ((0, 8), (1, 4)), (1, 0, 8, 2.0))
    gate_pre = scatter_about(splits[2], (TOKENS, FF), 1.0, 6.0, ((0, 4), (1, 8)))
    up_pre = scatter_about(splits[3], (TOKENS, FF), 1.0, 6.0, ((0, 4), (1, 8)))
    gate_weight = scatter_about(splits[4], (D, FF), D ** -0.5, 0.0625, ((0, 4), (1, 8)))
    up_weight = scatter_about(splits[5], (D, FF), D ** -0.5, 0.0625, ((0, 4), (1, 8)))
    down_weight = scatter_about(splits[6], (FF, D), D ** -0.5, 0.0625, ((0, 8), (1, 4)))
    return dict(inputs=inputs, out_grad=out_grad, gate_pre=gate_pre, up_pre=up_pre, gate_weight=gate_weight, up_weight=up_weight, down_weight=down_weight)


def derivatives(gate_pre, up_pre, hidden_grad):
    gate_f32 = gate_pre.astype(jnp.float32)
    up_f32 = up_pre.astype(jnp.float32)
    sigmoid = 1.0 / (1.0 + jnp.exp(-gate_f32))
    activated = gate_f32 * sigmoid
    hidden = (activated * up_f32).astype(jnp.bfloat16)
    gate_delta = (hidden_grad * up_f32 * sigmoid * (1.0 + gate_f32 * (1.0 - sigmoid))).astype(jnp.bfloat16)
    up_delta = (hidden_grad * activated).astype(jnp.bfloat16)
    return hidden, gate_delta, up_delta


def rounded(value):
    narrow = lax.optimization_barrier(value.astype(jnp.bfloat16))
    return narrow.astype(jnp.float32)


def reference(inputs, out_grad, gate_pre, up_pre, gate_weight, up_weight, down_weight):
    by_cols = (((1,), (1,)), ((), ()))
    by_rows = (((0,), (0,)), ((), ()))
    hidden_grad = jnp.zeros((TOKENS, FF), jnp.float32)
    for row_block in range(N_ROW):
        offset = row_block * D_BLK
        block_term = lax.dot_general(out_grad[:, offset:offset + D_BLK], down_weight[:, offset:offset + D_BLK], by_cols, preferred_element_type=jnp.float32)
        hidden_grad = hidden_grad + rounded(block_term)
    hidden, gate_delta, up_delta = derivatives(gate_pre, up_pre, hidden_grad)
    down_grad = lax.dot_general(hidden, out_grad, by_rows, preferred_element_type=jnp.float32).astype(jnp.bfloat16)
    gate_grad = lax.dot_general(inputs, gate_delta, by_rows, preferred_element_type=jnp.float32).astype(jnp.bfloat16)
    up_grad = lax.dot_general(inputs, up_delta, by_rows, preferred_element_type=jnp.float32).astype(jnp.bfloat16)
    input_sum = jnp.zeros((TOKENS, D), jnp.float32)
    for col_block in range(N_COL):
        offset = col_block * FF_BLK
        block_term = lax.dot_general(gate_delta[:, offset:offset + FF_BLK], gate_weight[:, offset:offset + FF_BLK], by_cols, preferred_element_type=jnp.float32)
        block_term = block_term + lax.dot_general(up_delta[:, offset:offset + FF_BLK], up_weight[:, offset:offset + FF_BLK], by_cols, preferred_element_type=jnp.float32)
        input_sum = input_sum + rounded(block_term)
    input_grad = input_sum.astype(jnp.bfloat16)
    return (input_grad, gate_grad, up_grad, down_grad)
```

```python
import functools

import jax
import jax.numpy as jnp
from jax import lax
from jax.experimental import pallas as pl
from jax.experimental.pallas import tpu as pltpu
from jax.sharding import PartitionSpec as P

BF16 = jnp.bfloat16
F32 = jnp.float32
MESH = pl.DeviceIdType.MESH
CHUNKS = 4
BY_COLS = (((1,), (1,)), ((), ()))
BY_ROWS = (((0,), (0,)), ((), ()))


class Ring:
    def __init__(self, name, size):
        self.name = name
        self.outers = size // 2
        self.index = lax.axis_index(name)
        self.pair = lax.rem(self.index, 2)
        self.outer = self.index // 2
        self.partner = self.outer * 2 + (1 - self.pair)

    def ahead(self, step):
        return lax.rem(self.outer + step, self.outers) * 2 + self.pair

    def behind_outer(self, step):
        return lax.rem(self.outer + self.outers - step, self.outers)

    def copy(self, src, dst, send_sem, recv_sem, target):
        return pltpu.make_async_remote_copy(
            src_ref=src,
            dst_ref=dst,
            send_sem=send_sem,
            recv_sem=recv_sem,
            device_id={self.name: target},
            device_id_type=MESH,
        )

    def everyone(self):
        return [self.partner] + [self.ahead(step) for step in range(1, self.outers)]


class Gather:
    def __init__(self, ring, held, send, recv):
        self.ring, self.held = ring, held
        n = ring.outers
        own = held.at[ring.index]
        self.direct = [
            ring.copy(own, own, send.at[s], recv.at[s], ring.ahead(s)) for s in range(1, n)
        ]
        self.relays = []
        for s in range(n):
            block = held.at[ring.behind_outer(s) * 2 + ring.pair]
            self.relays.append(
                ring.copy(block, block, send.at[n + s], recv.at[n + s], ring.partner)
            )

    def start(self):
        for copy in self.direct:
            copy.start()
        self.relays[0].start()

    def relay(self):
        for s in range(1, self.ring.outers):
            self.direct[s - 1].wait_recv()
            self.relays[s].start()

    def finish(self):
        for copy in self.relays:
            copy.wait_recv()

    def drain(self):
        for copy in self.direct + self.relays:
            copy.wait_send()


def main_kernel(
    n_row,
    n_col,
    inputs_ref,
    grads_ref,
    gate_ref,
    up_ref,
    gate_w_hbm,
    up_w_hbm,
    down_w_hbm,
    all_inputs_ref,
    all_grads_ref,
    hidden_ref,
    gate_delta_ref,
    up_delta_ref,
    input_grad_ref,
    held_grads,
    held_inputs,
    held_gate,
    held_up,
    gate_w,
    up_w,
    down_w,
    gate_factor,
    up_factor,
    pair_out,
    pair_in,
    own_half,
    outer_held,
    totals,
    part_out,
    part_in,
    part_own,
    sum_out,
    sum_in,
    load_sem,
    grads_send,
    grads_recv,
    inputs_send,
    inputs_recv,
    gate_send,
    gate_recv,
    up_send,
    up_recv,
    pair_send,
    pair_recv,
    outer_send,
    outer_recv,
    total_send,
    total_recv,
    part_send,
    part_recv,
    sum_send,
    sum_recv,
):
    row = Ring("row", n_row)
    col = Ring("col", n_col)
    rows_c, width = grads_ref.shape
    rows_r, hid = gate_ref.shape
    tokens = rows_c * n_col
    half = tokens // 2
    step_f = hid // CHUNKS
    step_d = width // CHUNKS
    outers_r, outers_c = row.outers, col.outers

    loads = []
    for j in range(CHUNKS):
        here = pl.ds(j * step_f, step_f)
        loads.append(pltpu.make_async_copy(down_w_hbm.at[here], down_w.at[here], load_sem.at[j]))
    for j in range(CHUNKS):
        here = pl.ds(j * step_d, step_d)
        loads.append(
            pltpu.make_async_copy(gate_w_hbm.at[here], gate_w.at[here], load_sem.at[CHUNKS + j])
        )
        loads.append(
            pltpu.make_async_copy(up_w_hbm.at[here], up_w.at[here], load_sem.at[2 * CHUNKS + j])
        )
    for load in loads:
        load.start()

    held_grads[col.index] = grads_ref[...]
    held_inputs[col.index] = inputs_ref[...]
    held_gate[row.index] = gate_ref[...]
    held_up[row.index] = up_ref[...]

    barrier = pltpu.get_barrier_semaphore()
    greeted = 0
    for ring in (row, col):
        for target in ring.everyone():
            pl.semaphore_signal(
                barrier, inc=1, device_id={ring.name: target}, device_id_type=MESH
            )
            greeted += 1
    pl.semaphore_wait(barrier, greeted)

    grads = Gather(col, held_grads, grads_send, grads_recv)
    gates = Gather(row, held_gate, gate_send, gate_recv)
    ups = Gather(row, held_up, up_send, up_recv)
    features = Gather(col, held_inputs, inputs_send, inputs_recv)
    grads.start()
    gates.start()
    ups.start()
    grads.relay()
    features.start()
    gates.relay()
    ups.relay()
    grads.finish()
    all_grads = held_grads[...].reshape(tokens, width)
    all_grads_ref[...] = all_grads

    def pair_copy(j):
        return row.copy(pair_out.at[j], pair_in.at[j], pair_send.at[j], pair_recv.at[j], row.partner)

    def outer_copy(j, s):
        own = outer_held.at[j, row.outer]
        return row.copy(own, own, outer_send.at[j, s], outer_recv.at[j, s], row.ahead(s))

    def total_copy(j):
        own = totals.at[j, row.pair]
        return row.copy(own, own, total_send.at[j], total_recv.at[j], row.partner)

    def hidden_part(j):
        loads[j].wait()
        part = lax.dot_general(
            held_grads[...].reshape(tokens, width),
            down_w[j * step_f : (j + 1) * step_f, :],
            BY_COLS,
            preferred_element_type=F32,
        )
        first, second = part[:half], part[half:]
        is_first = row.pair == 0
        pair_out[j] = jnp.where(is_first, second, first).astype(BF16)
        own_half[j] = jnp.where(is_first, first, second)
        pair_copy(j).start()

    def pair_sum(j):
        pair_copy(j).wait_recv()
        outer_held[j, row.outer] = (own_half[j] + pair_in[j].astype(F32)).astype(BF16)
        for s in range(1, outers_r):
            outer_copy(j, s).start()

    def outer_sum(j):
        for s in range(1, outers_r):
            outer_copy(j, s).wait_recv()
        total = outer_held[j, 0].astype(F32)
        for o in range(1, outers_r):
            total = total + outer_held[j, o].astype(F32)
        totals[j, row.pair] = total.astype(BF16)
        total_copy(j).start()

    def deltas(j):
        total_copy(j).wait_recv()
        here = slice(j * step_f, (j + 1) * step_f)
        total = totals[j].reshape(tokens, step_f).astype(F32)
        gate_delta_ref[:, here] = (total * gate_factor[:, here]).astype(BF16)
        up_delta_ref[:, here] = (total * up_factor[:, here]).astype(BF16)

    def activations():
        for r in range(n_row):
            here = slice(r * rows_r, (r + 1) * rows_r)
            gate_f32 = held_gate[r].astype(F32)
            up_f32 = held_up[r].astype(F32)
            sigmoid = 1.0 / (1.0 + jnp.exp(-gate_f32))
            activated = gate_f32 * sigmoid
            hidden_ref[here, :] = (activated * up_f32).astype(BF16)
            gate_factor[here, :] = up_f32 * sigmoid * (1.0 + gate_f32 * (1.0 - sigmoid))
            up_factor[here, :] = activated

    for j in range(CHUNKS):
        hidden_part(j)
        if j >= 1:
            pair_sum(j - 1)
    pair_sum(CHUNKS - 1)
    gates.finish()
    ups.finish()
    activations()
    features.relay()
    for j in range(CHUNKS):
        outer_sum(j)
        if j >= 1:
            deltas(j - 1)
    deltas(CHUNKS - 1)

    def part_copy(j):
        return col.copy(part_out.at[j], part_in.at[j], part_send.at[j], part_recv.at[j], col.partner)

    def sum_copy(j, s):
        target = col.ahead(s)
        return col.copy(
            sum_out.at[j, target // 2],
            sum_in.at[j, s],
            sum_send.at[j, s],
            sum_recv.at[j, s],
            target,
        )

    def input_part(j):
        loads[CHUNKS + 2 * j].wait()
        loads[CHUNKS + 2 * j + 1].wait()
        here = slice(j * step_d, (j + 1) * step_d)
        part = lax.dot_general(
            gate_delta_ref[...], gate_w[here, :], BY_COLS, preferred_element_type=F32
        ) + lax.dot_general(up_delta_ref[...], up_w[here, :], BY_COLS, preferred_element_type=F32)
        part = part.reshape(outers_c, 2, rows_c, step_d)
        even, odd = part[:, 0], part[:, 1]
        is_even = col.pair == 0
        part_out[j] = jnp.where(is_even, odd, even).astype(BF16)
        part_own[j] = jnp.where(is_even, even, odd)
        part_copy(j).start()

    def part_sum(j):
        part_copy(j).wait_recv()
        total = part_own[j] + part_in[j].astype(F32)
        part_own[j] = total
        sum_out[j] = total.astype(BF16)
        for s in range(1, outers_c):
            sum_copy(j, s).start()

    for j in range(CHUNKS):
        input_part(j)
        if j >= 1:
            part_sum(j - 1)
    part_sum(CHUNKS - 1)
    features.finish()
    all_inputs_ref[...] = held_inputs[...].reshape(tokens, width)
    for j in range(CHUNKS):
        total = part_own[j, col.outer]
        for s in range(1, outers_c):
            sum_copy(j, s).wait_recv()
            total = total + sum_in[j, s].astype(F32)
        input_grad_ref[:, j * step_d : (j + 1) * step_d] = total.astype(BF16)

    for gather in (grads, gates, ups, features):
        gather.drain()
    for j in range(CHUNKS):
        pair_copy(j).wait_send()
        total_copy(j).wait_send()
        part_copy(j).wait_send()
        for s in range(1, outers_r):
            outer_copy(j, s).wait_send()
        for s in range(1, outers_c):
            sum_copy(j, s).wait_send()


def main_call(n_row, n_col, inputs, out_grad, gate_pre, up_pre, gate_weight, up_weight, down_weight):
    rows_c, width = inputs.shape
    rows_r, hid = gate_pre.shape
    tokens = rows_c * n_col
    half = tokens // 2
    step_f, step_d = hid // CHUNKS, width // CHUNKS
    outers_r, outers_c = n_row // 2, n_col // 2
    vmem = pl.BlockSpec(memory_space=pltpu.VMEM)
    anywhere = pl.BlockSpec(memory_space=pl.ANY)
    dma = pltpu.SemaphoreType.DMA
    wide = jax.ShapeDtypeStruct((tokens, width), BF16)
    deep = jax.ShapeDtypeStruct((tokens, hid), BF16)
    gather_sems = [dma((n_col,))] * 4 + [dma((n_row,))] * 4
    return pl.pallas_call(
        functools.partial(main_kernel, n_row, n_col),
        out_shape=(wide, wide, deep, deep, deep, jax.ShapeDtypeStruct((rows_c, width), BF16)),
        in_specs=[vmem] * 4 + [anywhere] * 3,
        out_specs=[vmem] * 6,
        scratch_shapes=[
            pltpu.VMEM((n_col, rows_c, width), BF16),
            pltpu.VMEM((n_col, rows_c, width), BF16),
            pltpu.VMEM((n_row, rows_r, hid), BF16),
            pltpu.VMEM((n_row, rows_r, hid), BF16),
            pltpu.VMEM((width, hid), BF16),
            pltpu.VMEM((width, hid), BF16),
            pltpu.VMEM((hid, width), BF16),
            pltpu.VMEM((tokens, hid), F32),
            pltpu.VMEM((tokens, hid), F32),
            pltpu.VMEM((CHUNKS, half, step_f), BF16),
            pltpu.VMEM((CHUNKS, half, step_f), BF16),
            pltpu.VMEM((CHUNKS, half, step_f), F32),
            pltpu.VMEM((CHUNKS, outers_r, half, step_f), BF16),
            pltpu.VMEM((CHUNKS, 2, half, step_f), BF16),
            pltpu.VMEM((CHUNKS, outers_c, rows_c, step_d), BF16),
            pltpu.VMEM((CHUNKS, outers_c, rows_c, step_d), BF16),
            pltpu.VMEM((CHUNKS, outers_c, rows_c, step_d), F32),
            pltpu.VMEM((CHUNKS, outers_c, rows_c, step_d), BF16),
            pltpu.VMEM((CHUNKS, outers_c, rows_c, step_d), BF16),
            dma((3 * CHUNKS,)),
        ]
        + gather_sems
        + [dma((CHUNKS,)), dma((CHUNKS,))]
        + [dma((CHUNKS, outers_r)), dma((CHUNKS, outers_r))]
        + [dma((CHUNKS,)), dma((CHUNKS,))]
        + [dma((CHUNKS,)), dma((CHUNKS,))]
        + [dma((CHUNKS, outers_c)), dma((CHUNKS, outers_c))],
        compiler_params=pltpu.CompilerParams(
            collective_id=0, has_side_effects=True, vmem_limit_bytes=58 * 1024 * 1024
        ),
        cost_estimate=pl.CostEstimate(
            flops=6 * tokens * width * hid,
            bytes_accessed=6 * width * hid,
            transcendentals=tokens * hid,
        ),
        name="main",
    )(inputs, out_grad, gate_pre, up_pre, gate_weight, up_weight, down_weight)


def grads_kernel(
    inputs_ref, hidden_ref, gate_delta, up_delta, grads, gate_grad_ref, up_grad_ref, down_grad_ref
):
    def product(left, right):
        return lax.dot_general(left, right, BY_ROWS, preferred_element_type=F32).astype(BF16)

    left = inputs_ref[...]
    gate_grad_ref[...] = product(left, gate_delta[...])
    up_grad_ref[...] = product(left, up_delta[...])
    down_grad_ref[...] = product(hidden_ref[...], grads[...])


def grads_call(all_inputs, all_grads, hidden, gate_delta, up_delta):
    tokens, width = all_inputs.shape
    hid = hidden.shape[1]
    steps = min(8, width // 128, hid // 128)
    whole = pl.BlockSpec(memory_space=pltpu.VMEM)
    return pl.pallas_call(
        grads_kernel,
        grid=(steps,),
        out_shape=(
            jax.ShapeDtypeStruct((width, hid), BF16),
            jax.ShapeDtypeStruct((width, hid), BF16),
            jax.ShapeDtypeStruct((hid, width), BF16),
        ),
        in_specs=[
            pl.BlockSpec((tokens, width // steps), lambda i: (0, i)),
            pl.BlockSpec((tokens, hid // steps), lambda i: (0, i)),
            whole,
            whole,
            whole,
        ],
        out_specs=[
            pl.BlockSpec((width // steps, hid), lambda i: (i, 0)),
            pl.BlockSpec((width // steps, hid), lambda i: (i, 0)),
            pl.BlockSpec((hid // steps, width), lambda i: (i, 0)),
        ],
        compiler_params=pltpu.CompilerParams(vmem_limit_bytes=48 * 1024 * 1024),
        cost_estimate=pl.CostEstimate(
            flops=6 * tokens * width * hid,
            bytes_accessed=6 * width * hid,
            transcendentals=0,
        ),
        name="weight_grads",
    )(all_inputs, hidden, gate_delta, up_delta, all_grads)


def solution(mesh):
    n_row, n_col = mesh.shape["row"], mesh.shape["col"]

    def per_device(inputs, out_grad, gate_pre, up_pre, gate_weight, up_weight, down_weight):
        all_inputs, all_grads, hidden, gate_delta, up_delta, input_grad = main_call(
            n_row, n_col, inputs, out_grad, gate_pre, up_pre, gate_weight, up_weight, down_weight
        )
        gate_grad, up_grad, down_grad = grads_call(
            all_inputs, all_grads, hidden, gate_delta, up_delta
        )
        return (input_grad, gate_grad, up_grad, down_grad)

    in_specs = (
        P("col", "row"),
        P("col", "row"),
        P("row", "col"),
        P("row", "col"),
        P("row", "col"),
        P("row", "col"),
        P("col", "row"),
    )
    out_specs = (P("col", "row"), P("row", "col"), P("row", "col"), P("col", "row"))
    return jax.shard_map(
        per_device, mesh=mesh, in_specs=in_specs, out_specs=out_specs, check_vma=False
    )
```

```python
import functools

import jax
import jax.numpy as jnp
from jax import lax
from jax.experimental import pallas as pl
from jax.experimental.pallas import tpu as pltpu
from jax.sharding import PartitionSpec as P

BF16 = jnp.bfloat16
F32 = jnp.float32
MESH = pl.DeviceIdType.MESH
CHUNKS = 2
BY_COLS = (((1,), (1,)), ((), ()))
BY_ROWS = (((0,), (0,)), ((), ()))


class Ring:
    def __init__(self, name, size):
        self.name = name
        self.outers = size // 2
        self.index = lax.axis_index(name)
        self.pair = lax.rem(self.index, 2)
        self.outer = self.index // 2
        self.partner = self.outer * 2 + (1 - self.pair)

    def ahead(self, step):
        return lax.rem(self.outer + step, self.outers) * 2 + self.pair

    def behind_outer(self, step):
        return lax.rem(self.outer + self.outers - step, self.outers)

    def copy(self, src, dst, send_sem, recv_sem, target):
        return pltpu.make_async_remote_copy(
            src_ref=src,
            dst_ref=dst,
            send_sem=send_sem,
            recv_sem=recv_sem,
            device_id={self.name: target},
            device_id_type=MESH,
        )

    def everyone(self):
        return [self.partner] + [self.ahead(step) for step in range(1, self.outers)]


class Gather:
    def __init__(self, ring, held, send, recv):
        self.ring, self.held = ring, held
        n = ring.outers
        own = held.at[ring.index]
        self.direct = [
            ring.copy(own, own, send.at[s], recv.at[s], ring.ahead(s)) for s in range(1, n)
        ]
        self.relays = []
        for s in range(n):
            block = held.at[ring.behind_outer(s) * 2 + ring.pair]
            self.relays.append(
                ring.copy(block, block, send.at[n + s], recv.at[n + s], ring.partner)
            )

    def start(self):
        for copy in self.direct:
            copy.start()
        self.relays[0].start()

    def relay(self):
        for s in range(1, self.ring.outers):
            self.direct[s - 1].wait_recv()
            self.relays[s].start()

    def finish(self):
        for copy in self.relays:
            copy.wait_recv()

    def drain(self):
        for copy in self.direct + self.relays:
            copy.wait_send()


def main_kernel(
    n_row,
    n_col,
    inputs_ref,
    grads_ref,
    gate_ref,
    up_ref,
    gate_w_hbm,
    up_w_hbm,
    down_w_hbm,
    all_inputs_ref,
    all_grads_ref,
    hidden_ref,
    gate_delta_ref,
    up_delta_ref,
    input_grad_ref,
    held_grads,
    held_inputs,
    held_gate,
    held_up,
    gate_w,
    up_w,
    down_w,
    gate_factor,
    up_factor,
    pair_out,
    pair_in,
    own_half,
    outer_held,
    totals,
    part_out,
    part_in,
    part_own,
    sum_out,
    sum_in,
    load_sem,
    grads_send,
    grads_recv,
    inputs_send,
    inputs_recv,
    gate_send,
    gate_recv,
    up_send,
    up_recv,
    pair_send,
    pair_recv,
    outer_send,
    outer_recv,
    total_send,
    total_recv,
    part_send,
    part_recv,
    sum_send,
    sum_recv,
):
    row = Ring("row", n_row)
    col = Ring("col", n_col)
    rows_c, width = grads_ref.shape
    rows_r, hid = gate_ref.shape
    tokens = rows_c * n_col
    half = tokens // 2
    step_f = hid // CHUNKS
    step_d = width // CHUNKS
    outers_r, outers_c = row.outers, col.outers

    loads = []
    for j in range(CHUNKS):
        here = pl.ds(j * step_f, step_f)
        loads.append(pltpu.make_async_copy(down_w_hbm.at[here], down_w.at[here], load_sem.at[j]))
    for j in range(CHUNKS):
        here = pl.ds(j * step_d, step_d)
        loads.append(
            pltpu.make_async_copy(gate_w_hbm.at[here], gate_w.at[here], load_sem.at[CHUNKS + j])
        )
        loads.append(
            pltpu.make_async_copy(up_w_hbm.at[here], up_w.at[here], load_sem.at[2 * CHUNKS + j])
        )
    for load in loads:
        load.start()

    held_grads[col.index] = grads_ref[...]
    held_inputs[col.index] = inputs_ref[...]
    held_gate[row.index] = gate_ref[...]
    held_up[row.index] = up_ref[...]

    barrier = pltpu.get_barrier_semaphore()
    greeted = 0
    for ring in (row, col):
        for target in ring.everyone():
            pl.semaphore_signal(
                barrier, inc=1, device_id={ring.name: target}, device_id_type=MESH
            )
            greeted += 1
    pl.semaphore_wait(barrier, greeted)

    def activations():
        for r in range(n_row):
            here = slice(r * rows_r, (r + 1) * rows_r)
            gate_f32 = held_gate[r].astype(F32)
            up_f32 = held_up[r].astype(F32)
            sigmoid = 1.0 / (1.0 + jnp.exp(-gate_f32))
            activated = gate_f32 * sigmoid
            hidden_ref[here, :] = (activated * up_f32).astype(BF16)
            gate_factor[here, :] = up_f32 * sigmoid * (1.0 + gate_f32 * (1.0 - sigmoid))
            up_factor[here, :] = activated

    grads = Gather(col, held_grads, grads_send, grads_recv)
    gates = Gather(row, held_gate, gate_send, gate_recv)
    ups = Gather(row, held_up, up_send, up_recv)
    features = Gather(col, held_inputs, inputs_send, inputs_recv)
    grads.start()
    gates.start()
    ups.start()
    grads.relay()
    features.start()
    gates.relay()
    ups.relay()
    gates.finish()
    ups.finish()
    activations()
    grads.finish()
    all_grads = held_grads[...].reshape(tokens, width)
    all_grads_ref[...] = all_grads

    def pair_copy(j):
        return row.copy(pair_out.at[j], pair_in.at[j], pair_send.at[j], pair_recv.at[j], row.partner)

    def outer_copy(j, s):
        own = outer_held.at[j, row.outer]
        return row.copy(own, own, outer_send.at[j, s], outer_recv.at[j, s], row.ahead(s))

    def total_copy(j):
        own = totals.at[j, row.pair]
        return row.copy(own, own, total_send.at[j], total_recv.at[j], row.partner)

    def hidden_part(j):
        loads[j].wait()
        part = lax.dot_general(
            held_grads[...].reshape(tokens, width),
            down_w[j * step_f : (j + 1) * step_f, :],
            BY_COLS,
            preferred_element_type=F32,
        )
        first, second = part[:half], part[half:]
        is_first = row.pair == 0
        pair_out[j] = jnp.where(is_first, second, first).astype(BF16)
        own_half[j] = jnp.where(is_first, first, second)
        pair_copy(j).start()

    def pair_sum(j):
        pair_copy(j).wait_recv()
        outer_held[j, row.outer] = (own_half[j] + pair_in[j].astype(F32)).astype(BF16)
        for s in range(1, outers_r):
            outer_copy(j, s).start()

    def outer_sum(j):
        for s in range(1, outers_r):
            outer_copy(j, s).wait_recv()
        total = outer_held[j, 0].astype(F32)
        for o in range(1, outers_r):
            total = total + outer_held[j, o].astype(F32)
        totals[j, row.pair] = total.astype(BF16)
        total_copy(j).start()

    def deltas(j):
        total_copy(j).wait_recv()
        here = slice(j * step_f, (j + 1) * step_f)
        total = totals[j].reshape(tokens, step_f).astype(F32)
        gate_delta_ref[:, here] = (total * gate_factor[:, here]).astype(BF16)
        up_delta_ref[:, here] = (total * up_factor[:, here]).astype(BF16)

    for j in range(CHUNKS):
        hidden_part(j)
        if j >= 1:
            pair_sum(j - 1)
    pair_sum(CHUNKS - 1)
    features.relay()
    for j in range(CHUNKS):
        outer_sum(j)
        if j >= 1:
            deltas(j - 1)
    deltas(CHUNKS - 1)

    def part_copy(j):
        return col.copy(part_out.at[j], part_in.at[j], part_send.at[j], part_recv.at[j], col.partner)

    def sum_copy(j, s):
        target = col.ahead(s)
        return col.copy(
            sum_out.at[j, target // 2],
            sum_in.at[j, s],
            sum_send.at[j, s],
            sum_recv.at[j, s],
            target,
        )

    def input_part(j):
        loads[CHUNKS + 2 * j].wait()
        loads[CHUNKS + 2 * j + 1].wait()
        here = slice(j * step_d, (j + 1) * step_d)
        part = lax.dot_general(
            gate_delta_ref[...], gate_w[here, :], BY_COLS, preferred_element_type=F32
        ) + lax.dot_general(up_delta_ref[...], up_w[here, :], BY_COLS, preferred_element_type=F32)
        part = part.reshape(outers_c, 2, rows_c, step_d)
        even, odd = part[:, 0], part[:, 1]
        is_even = col.pair == 0
        part_out[j] = jnp.where(is_even, odd, even).astype(BF16)
        part_own[j] = jnp.where(is_even, even, odd)
        part_copy(j).start()

    def part_sum(j):
        part_copy(j).wait_recv()
        total = part_own[j] + part_in[j].astype(F32)
        part_own[j] = total
        sum_out[j] = total.astype(BF16)
        for s in range(1, outers_c):
            sum_copy(j, s).start()

    for j in range(CHUNKS):
        input_part(j)
        if j >= 1:
            part_sum(j - 1)
    part_sum(CHUNKS - 1)
    features.finish()
    all_inputs_ref[...] = held_inputs[...].reshape(tokens, width)
    for j in range(CHUNKS):
        total = part_own[j, col.outer]
        for s in range(1, outers_c):
            sum_copy(j, s).wait_recv()
            total = total + sum_in[j, s].astype(F32)
        input_grad_ref[:, j * step_d : (j + 1) * step_d] = total.astype(BF16)

    for gather in (grads, gates, ups, features):
        gather.drain()
    for j in range(CHUNKS):
        pair_copy(j).wait_send()
        total_copy(j).wait_send()
        part_copy(j).wait_send()
        for s in range(1, outers_r):
            outer_copy(j, s).wait_send()
        for s in range(1, outers_c):
            sum_copy(j, s).wait_send()


def main_call(n_row, n_col, inputs, out_grad, gate_pre, up_pre, gate_weight, up_weight, down_weight):
    rows_c, width = inputs.shape
    rows_r, hid = gate_pre.shape
    tokens = rows_c * n_col
    half = tokens // 2
    step_f, step_d = hid // CHUNKS, width // CHUNKS
    outers_r, outers_c = n_row // 2, n_col // 2
    vmem = pl.BlockSpec(memory_space=pltpu.VMEM)
    anywhere = pl.BlockSpec(memory_space=pltpu.HBM)
    dma = pltpu.SemaphoreType.DMA
    wide = jax.ShapeDtypeStruct((tokens, width), BF16)
    deep = jax.ShapeDtypeStruct((tokens, hid), BF16)
    gather_sems = [dma((n_col,))] * 4 + [dma((n_row,))] * 4
    return pl.pallas_call(
        functools.partial(main_kernel, n_row, n_col),
        out_shape=(wide, wide, deep, deep, deep, jax.ShapeDtypeStruct((rows_c, width), BF16)),
        in_specs=[vmem] * 4 + [anywhere] * 3,
        out_specs=[vmem] * 6,
        scratch_shapes=[
            pltpu.VMEM((n_col, rows_c, width), BF16),
            pltpu.VMEM((n_col, rows_c, width), BF16),
            pltpu.VMEM((n_row, rows_r, hid), BF16),
            pltpu.VMEM((n_row, rows_r, hid), BF16),
            pltpu.VMEM((width, hid), BF16),
            pltpu.VMEM((width, hid), BF16),
            pltpu.VMEM((hid, width), BF16),
            pltpu.VMEM((tokens, hid), F32),
            pltpu.VMEM((tokens, hid), F32),
            pltpu.VMEM((CHUNKS, half, step_f), BF16),
            pltpu.VMEM((CHUNKS, half, step_f), BF16),
            pltpu.VMEM((CHUNKS, half, step_f), F32),
            pltpu.VMEM((CHUNKS, outers_r, half, step_f), BF16),
            pltpu.VMEM((CHUNKS, 2, half, step_f), BF16),
            pltpu.VMEM((CHUNKS, outers_c, rows_c, step_d), BF16),
            pltpu.VMEM((CHUNKS, outers_c, rows_c, step_d), BF16),
            pltpu.VMEM((CHUNKS, outers_c, rows_c, step_d), F32),
            pltpu.VMEM((CHUNKS, outers_c, rows_c, step_d), BF16),
            pltpu.VMEM((CHUNKS, outers_c, rows_c, step_d), BF16),
            dma((3 * CHUNKS,)),
        ]
        + gather_sems
        + [dma((CHUNKS,)), dma((CHUNKS,))]
        + [dma((CHUNKS, outers_r)), dma((CHUNKS, outers_r))]
        + [dma((CHUNKS,)), dma((CHUNKS,))]
        + [dma((CHUNKS,)), dma((CHUNKS,))]
        + [dma((CHUNKS, outers_c)), dma((CHUNKS, outers_c))],
        compiler_params=pltpu.CompilerParams(
            collective_id=0, has_side_effects=True, vmem_limit_bytes=58 * 1024 * 1024
        ),
        cost_estimate=pl.CostEstimate(
            flops=6 * tokens * width * hid,
            bytes_accessed=6 * width * hid,
            transcendentals=tokens * hid,
        ),
        name="main",
    )(inputs, out_grad, gate_pre, up_pre, gate_weight, up_weight, down_weight)


def grads_kernel(
    inputs_ref, hidden_ref, gate_delta, up_delta, grads, gate_grad_ref, up_grad_ref, down_grad_ref
):
    def product(left, right):
        return lax.dot_general(left, right, BY_ROWS, preferred_element_type=F32).astype(BF16)

    left = inputs_ref[...]
    gate_grad_ref[...] = product(left, gate_delta[...])
    up_grad_ref[...] = product(left, up_delta[...])
    down_grad_ref[...] = product(hidden_ref[...], grads[...])


def grads_call(all_inputs, all_grads, hidden, gate_delta, up_delta):
    tokens, width = all_inputs.shape
    hid = hidden.shape[1]
    steps = min(4, width // 128, hid // 128)
    deep = pl.BlockSpec((tokens, hid), lambda i: (0, 0))
    wide = pl.BlockSpec((tokens, width), lambda i: (0, 0))
    return pl.pallas_call(
        grads_kernel,
        grid=(steps,),
        out_shape=(
            jax.ShapeDtypeStruct((width, hid), BF16),
            jax.ShapeDtypeStruct((width, hid), BF16),
            jax.ShapeDtypeStruct((hid, width), BF16),
        ),
        in_specs=[
            pl.BlockSpec((tokens, width // steps), lambda i: (0, i)),
            pl.BlockSpec((tokens, hid // steps), lambda i: (0, i)),
            deep,
            deep,
            wide,
        ],
        out_specs=[
            pl.BlockSpec((width // steps, hid), lambda i: (i, 0)),
            pl.BlockSpec((width // steps, hid), lambda i: (i, 0)),
            pl.BlockSpec((hid // steps, width), lambda i: (i, 0)),
        ],
        compiler_params=pltpu.CompilerParams(vmem_limit_bytes=58 * 1024 * 1024),
        cost_estimate=pl.CostEstimate(
            flops=6 * tokens * width * hid,
            bytes_accessed=6 * width * hid,
            transcendentals=0,
        ),
        name="weight_grads",
    )(all_inputs, hidden, gate_delta, up_delta, all_grads)


def solution(mesh):
    n_row, n_col = mesh.shape["row"], mesh.shape["col"]

    def per_device(inputs, out_grad, gate_pre, up_pre, gate_weight, up_weight, down_weight):
        all_inputs, all_grads, hidden, gate_delta, up_delta, input_grad = main_call(
            n_row, n_col, inputs, out_grad, gate_pre, up_pre, gate_weight, up_weight, down_weight
        )
        gate_grad, up_grad, down_grad = grads_call(
            all_inputs, all_grads, hidden, gate_delta, up_delta
        )
        return (input_grad, gate_grad, up_grad, down_grad)

    in_specs = (
        P("col", "row"),
        P("col", "row"),
        P("row", "col"),
        P("row", "col"),
        P("row", "col"),
        P("row", "col"),
        P("col", "row"),
    )
    out_specs = (P("col", "row"), P("row", "col"), P("row", "col"), P("col", "row"))
    return jax.shard_map(
        per_device, mesh=mesh, in_specs=in_specs, out_specs=out_specs, check_vma=False
    )
```
